256 devices in a mesh: col: 16 (over z, core), row: 16 (over x, y).
Axes of the slice: x: 4, y: 4, z: 8, core: 2. Of those that a mesh axis runs over, the one named last changes fastest.
Arguments:
- top_sources: bfloat16 [14, 256, 256], P(None, 'row', 'col'), may hold values from -6 to 6
- leaf_sources: bfloat16 [2048, 256, 256], P(('col', 'row')), may hold values from -6 to 6
- top_inverse: bfloat16 [14, 256, 256], P(None, 'row'), may hold values from -1 to 4
- leaf_inverse: bfloat16 [2048, 256, 256], P(('col', 'row')), may hold values from -1 to 4
- top_coupling: bfloat16 [12, 6, 256, 256], P(None, None, 'row'), may hold values from -0.1875 to 0.1875
- leaf_coupling: bfloat16 [2048, 9, 256, 256], P(('col', 'row')), may hold values from -0.125 to 0.125
- leaf_links: int32 [2048, 9], P(('col', 'row')), may hold values from 0 to 13, as said below
Outputs:
- top_adjoint: bfloat16 [14, 256, 256], P(None, 'row', 'col')
- leaf_adjoint: bfloat16 [2048, 256, 256], P(('col', 'row'))
The draws below stay inside these ranges and needn't reach their ends.
Inputs may be any that keep to these rules, and one draw needn't show every extreme that they name: `leaf_links`: entries 0 to 1 of a row name distinct blocks of level 0, the next 3 distinct blocks of level 1, the last 4 distinct blocks of level 2.
All inputs are finite; a program needn't handle non-finite values.
Results may differ from the reference program's by a relative error of at most 0.0072.
Values may be sent and summed in bfloat16 or wider, within the bound.
A program may use at most 128 MiB of HBM per device.

```python
import math
import jax
import jax.numpy as jnp
from jax import lax

BLOCK = 256
SOURCES = 256
LEVEL0 = 2
LEVEL1 = 4
LEVEL2 = 8
LINKS0 = 2
LINKS1 = 3
LINKS2 = 4
TOP = 14
LINKS = 9
LEAVES = 2048


def inverse_law(key, count, diag_low, diag_high, off_scale, scale_low, scale_high):
    key_diag, key_off, key_rows = jax.random.split(key, 3)
    diagonal = jax.random.uniform(key_diag, (count, BLOCK), jnp.float32, diag_low, diag_high)
    offdiag = jax.random.uniform(key_off, (count, BLOCK, BLOCK), jnp.float32, -1.0, 1.0) * (off_scale / math.sqrt(BLOCK))
    row_scale = jnp.exp(jax.random.uniform(key_rows, (count, BLOCK, 1), jnp.float32, math.log(scale_low), math.log(scale_high)))
    identity = jnp.eye(BLOCK, dtype=jnp.float32)
    return ((identity[None, :, :] * diagonal[:, :, None] + offdiag) * row_scale).astype(jnp.bfloat16)


def draw_top_inverse(key, part):
    key = jax.random.fold_in(key, 11)
    return inverse_law(key, TOP, 0.8, 1.2, 0.9, 1.0, 1.0)


def draw_leaf_inverse(key, part):
    key = jax.random.fold_in(key, 13)
    return inverse_law(key, LEAVES, 0.8, 1.2, 0.9, 1.0, 1.0)


def draw_leaf_links(key, part):
    key = jax.random.fold_in(key, 23)
    block_starts = (0, LEVEL0, LEVEL0 + LEVEL1)
    block_counts = (LEVEL0, LEVEL1, LEVEL2)
    link_counts = (LINKS0, LINKS1, LINKS2)
    columns = []
    for tree_level in range(3):
        level_key = jax.random.fold_in(key, tree_level)
        count = block_counts[tree_level]
        scores = jax.random.randint(level_key, (LEAVES, count), 0, 1 << 20, jnp.int32) * count
        scores = scores + jnp.arange(count, dtype=jnp.int32)[None, :]
        order = jnp.argsort(scores, axis=1)[:, :link_counts[tree_level]].astype(jnp.int32)
        columns.append(order + block_starts[tree_level])
    return jnp.concatenate(columns, axis=1).astype(jnp.int32)


def block_levels(key, shape, shards, least, high):
    gain, own = 1.0, jax.random.fold_in(key, 6)
    for position, shards_of in shards:
        draws = jnp.exp(jax.random.uniform(jax.random.fold_in(own, position), (shards_of,), jnp.float32, least / len(shards), high / len(shards)))
        gain = gain * jnp.repeat(draws, shape[position] // shards_of).reshape([-1 if axis == position else 1 for axis in range(len(shape))])
    return gain


def bell_draw(rng, dims, deviation, bound, pieces=(), kind=jnp.bfloat16):
    drawn = deviation * jax.random.normal(rng, dims, jnp.float32)
    if pieces:
        drawn = drawn * block_levels(rng, dims, pieces, -0.22, 0.18)
    return jnp.clip(drawn, -bound, bound).astype(kind)


def setup_inputs(seed: int = 0) -> dict:
    splits = jax.random.split(jax.random.key(seed), 8)
    top_sources = bell_draw(splits[0], (TOP, BLOCK, SOURCES), 1.0, 6.0, ((1, 16), (2, 16)))
    leaf_sources = bell_draw(splits[1], (LEAVES, BLOCK, SOURCES), 1.0, 6.0, ((0, 256),))
    top_inverse = draw_top_inverse(jax.random.fold_in(splits[7], 71), 0)
    leaf_inverse = draw_leaf_inverse(jax.random.fold_in(splits[7], 71), 0)
    top_coupling = bell_draw(splits[4], (LEVEL1 + LEVEL2, LEVEL0 + LEVEL1, BLOCK, BLOCK), (4 * BLOCK) ** -0.5, 0.1875, ((2, 16),))
    leaf_coupling = bell_draw(splits[5], (LEAVES, LINKS, BLOCK, BLOCK), (LINKS * BLOCK) ** -0.5, 0.125, ((0, 256),))
    leaf_links = draw_leaf_links(jax.random.fold_in(splits[7], 71), 0)
    return dict(top_sources=top_sources, leaf_sources=leaf_sources, top_inverse=top_inverse, leaf_inverse=leaf_inverse, top_coupling=top_coupling, leaf_coupling=leaf_coupling, leaf_links=leaf_links)


def reference(top_sources, leaf_sources, top_inverse, leaf_inverse, top_coupling, leaf_coupling, leaf_links):
    block_starts = (0, LEVEL0, LEVEL0 + LEVEL1)
    block_counts = (LEVEL0, LEVEL1, LEVEL2)
    solved = []
    for tree_level in range(3):
        start_block = block_starts[tree_level]
        stop_block = start_block + block_counts[tree_level]
        update = jnp.zeros((block_counts[tree_level], BLOCK, SOURCES), jnp.float32)
        if tree_level > 0:
            earlier = jnp.concatenate(solved, axis=0).astype(jnp.float32)
            coupling = top_coupling[start_block - LEVEL0:stop_block - LEVEL0, :start_block].astype(jnp.float32)
            update = jnp.einsum("jbrs,bsc->jrc", coupling, earlier)
        residual = (top_sources[start_block:stop_block].astype(jnp.float32) - update).astype(jnp.bfloat16)
        adjoint = jnp.einsum("jrs,jsc->jrc", top_inverse[start_block:stop_block].astype(jnp.float32),
                             residual.astype(jnp.float32)).astype(jnp.bfloat16)
        solved.append(adjoint)
    top_adjoint = jnp.concatenate(solved, axis=0)

    def one_leaf(item):
        coupling, sources, inverse, links = item
        picked = jnp.take(top_adjoint, links.astype(jnp.int32), axis=0).astype(jnp.float32)
        update = jnp.einsum("qrs,qsc->rc", coupling.astype(jnp.float32), picked)
        residual = (sources.astype(jnp.float32) - update).astype(jnp.bfloat16)
        return jnp.dot(inverse, residual, preferred_element_type=jnp.float32).astype(jnp.bfloat16)

    leaf_adjoint = lax.map(one_leaf, (leaf_coupling, leaf_sources, leaf_inverse, leaf_links))
    return top_adjoint, leaf_adjoint
```

```python
import jax
import jax.numpy as jnp
from jax import lax
from jax.experimental import pallas as pl
from jax.experimental.pallas import tpu as pltpu
from jax.sharding import PartitionSpec as P

LEVEL0 = 2
LEVEL1 = 4
LEVEL2 = 8
EARLY = LEVEL0 + LEVEL1
TOP = EARLY + LEVEL2
EARLY_LINKS = 5
LINKS = 9
LEAVES = 8
BLOCK = 256
HALF = 128
ROWS = 16
WIDTH = 16
PLANE = 16
DEPTH = 8
MESH = pl.DeviceIdType.MESH
BF16 = jnp.bfloat16
F32 = jnp.float32


def dot(a, b):
    return jnp.dot(a, b, preferred_element_type=F32)


def kernel(
    links,
    top_sources,
    leaf_sources,
    top_inverse,
    leaf_inverse,
    top_coupling,
    leaf_coupling,
    top_out,
    leaf_out,
    src_own,
    pack,
    zbuf,
    src_rows,
    sources,
    inv0,
    inv1,
    inv2,
    coup1,
    coup2,
    early,
    late,
    res_rows,
    residual,
    coupling,
    inverse,
    leaf_src,
    update,
    leaf_res,
    top_res,
    local_sem,
    send_sem,
    recv_sem,
    core_send,
    core_recv,
    leaf_sem,
    out_sem,
):
    col, row = lax.axis_index("col"), lax.axis_index("row")
    z, k = col // 2, lax.rem(col, 2)
    own = pl.multiple_of(row * ROWS, ROWS)
    rows = pl.ds(own, ROWS)
    other = (z * 2 + 1 - k, row)

    def row_peer(d):
        return (col, lax.rem(row + d, PLANE))

    first = pltpu.make_async_copy(top_sources, src_own, local_sem.at[0])
    first.start()
    barrier = pltpu.get_barrier_semaphore()

    def greet(d, carry):
        pl.semaphore_signal(barrier, 1, device_id=row_peer(d), device_id_type=MESH)
        pl.semaphore_signal(
            barrier, 1, device_id=(lax.rem(col + d, PLANE), row), device_id_type=MESH
        )
        return carry

    lax.fori_loop(1, PLANE, greet, 0)
    second = pltpu.make_async_copy(top_coupling.at[pl.ds(LEVEL1, LEVEL2)], coup2, local_sem.at[1])
    second.start()

    half0 = pl.ds(k, 1)
    half1 = pl.ds(LEVEL0 + 2 * k, 2)
    half2 = pl.ds(EARLY + 4 * k, 4)
    pairs = pl.ds(2 * k, 2)
    early_pairs = pl.ds(0, LEVEL0)
    groups = (
        (top_inverse.at[half0], lambda at: inv0.at[half0, at]),
        (
            top_coupling.at[pairs, early_pairs],
            lambda at: coup1.at[pairs, :, at],
        ),
        (top_inverse.at[half1], lambda at: inv1.at[pairs, at]),
        (top_inverse.at[half2], lambda at: inv2.at[pl.ds(4 * k, 4), at]),
    )
    for g, (source, place) in enumerate(groups):
        pltpu.make_async_copy(source, place(rows), recv_sem.at[g]).start()

    first.wait()
    lane = lax.broadcasted_iota(jnp.int32, (WIDTH, BLOCK), 1)
    repeat = (lax.rem(lane, WIDTH) == lax.broadcasted_iota(jnp.int32, (WIDTH, BLOCK), 0)).astype(
        F32
    ).astype(BF16)
    spread = dot(src_own[...].reshape(TOP * ROWS, WIDTH), repeat)
    place_row = lax.broadcasted_iota(jnp.int32, (TOP * ROWS, BLOCK), 0) // ROWS
    place_lane = lax.broadcasted_iota(jnp.int32, (TOP * ROWS, BLOCK), 1) // WIDTH
    spread = jnp.where(place_row == place_lane, spread, 0.0)
    pack[...] = spread.reshape(TOP, ROWS, BLOCK).sum(axis=0).astype(BF16)

    pl.semaphore_wait(barrier, 2 * (PLANE - 1))

    zhalf = z // 4
    slot = lax.rem(col, 8)

    def send_z(d, carry):
        pltpu.make_async_remote_copy(
            src_ref=pack,
            dst_ref=zbuf.at[slot],
            send_sem=send_sem.at[4],
            recv_sem=recv_sem.at[4],
            device_id=(lax.rem(z + d, DEPTH) * 2 + zhalf, row),
            device_id_type=MESH,
        ).start()
        return carry

    @pl.when(k == zhalf)
    def _():
        pltpu.make_async_copy(pack, zbuf.at[slot], recv_sem.at[4]).start()

    @pl.when(k != zhalf)
    def _():
        pltpu.make_async_remote_copy(
            src_ref=pack,
            dst_ref=zbuf.at[slot],
            send_sem=send_sem.at[7],
            recv_sem=recv_sem.at[4],
            device_id=other,
            device_id_type=MESH,
        ).start()

    lax.fori_loop(1, DEPTH, send_z, 0)

    def gather(g, source, target):
        def send(d, carry):
            pltpu.make_async_remote_copy(
                src_ref=source,
                dst_ref=target,
                send_sem=send_sem.at[g],
                recv_sem=recv_sem.at[g],
                device_id=row_peer(d),
                device_id_type=MESH,
            ).start()
            return carry

        lax.fori_loop(1, PLANE, send, 0)

    for g in range(3):
        gather(g, groups[g][0], groups[g][1](rows))

    leaf_copies = (
        pltpu.make_async_copy(leaf_sources, leaf_src, leaf_sem.at[0]),
        pltpu.make_async_copy(leaf_coupling, coupling, leaf_sem.at[1]),
        pltpu.make_async_copy(leaf_inverse, inverse, leaf_sem.at[2]),
    )
    for copy in leaf_copies:
        copy.start()

    pltpu.make_async_copy(zbuf, zbuf, recv_sem.at[4]).wait()
    square = (HALF, HALF)
    from_lane = lax.broadcasted_iota(jnp.int32, square, 0)
    to_lane = lax.broadcasted_iota(jnp.int32, square, 1)
    keep = from_lane // ROWS == to_lane // WIDTH
    collected = zbuf[...].reshape(HALF, BLOCK)
    for j in range(TOP):
        pick = (from_lane == lax.rem(to_lane, WIDTH) + WIDTH * (j % 8)).astype(F32).astype(BF16)
        moved = dot(collected[:, HALF * (j // 8) : HALF * (j // 8 + 1)], pick)
        moved = jnp.where(keep, moved, 0.0).reshape(DEPTH, ROWS, HALF).sum(axis=0).astype(BF16)
        src_rows[j] = moved
    early_rows = src_rows.at[pl.ds(0, EARLY)]
    pltpu.make_async_copy(early_rows, sources.at[:, rows], recv_sem.at[5]).start()
    gather(5, early_rows, sources.at[:, rows])
    gather(3, groups[3][0], groups[3][1](rows))

    halves = (
        inv0.at[half0],
        coup1.at[pairs],
        inv1.at[pairs],
        inv2.at[pl.ds(4 * k, 4)],
    )

    def share(g, part):
        copy = pltpu.make_async_remote_copy(
            src_ref=part,
            dst_ref=part,
            send_sem=core_send.at[g],
            recv_sem=core_recv.at[g],
            device_id=other,
            device_id_type=MESH,
        )
        copy.start()
        return copy

    shared = []
    for g in range(3):
        pltpu.make_async_copy(halves[g], halves[g], recv_sem.at[g]).wait()
        shared.append(share(g, halves[g]))

    shared[0].wait_recv()
    pltpu.make_async_copy(sources, sources, recv_sem.at[5]).wait()
    for b in range(LEVEL0):
        early[k, b] = dot(inv0[b], sources[b]).astype(BF16)
    shared[1].wait_recv()
    shared[2].wait_recv()
    for j in range(LEVEL1):
        total = dot(coup1[j, 0], early[k, 0]) + dot(coup1[j, 1], early[k, 1])
        rest = (sources[LEVEL0 + j].astype(F32) - total).astype(BF16)
        early[k, LEVEL0 + j] = dot(inv1[j], rest).astype(BF16)

    second.wait()
    total = jnp.zeros((LEVEL2 * ROWS, HALF), F32)
    for b in range(EARLY):
        total = total + dot(coup2[:, b].reshape(LEVEL2 * ROWS, BLOCK), early[k, b])
    late_src = src_rows[pl.ds(EARLY, LEVEL2)].astype(F32)
    res_rows[...] = (late_src - total.reshape(LEVEL2, ROWS, HALF)).astype(BF16)
    pltpu.make_async_copy(res_rows, residual.at[:, rows], recv_sem.at[6]).start()
    gather(6, res_rows, residual.at[:, rows])
    shared.append(share(4, early.at[k]))
    pltpu.make_async_copy(halves[3], halves[3], recv_sem.at[3]).wait()
    shared.append(share(3, halves[3]))

    shared[3].wait_recv()
    for copy in leaf_copies:
        copy.wait()

    def early_leaf(i, carry):
        total = leaf_src[i].astype(F32)
        for q in range(EARLY_LINKS):
            at = links[i, q]
            picked = jnp.concatenate([early[0, at], early[1, at]], axis=1)
            total = total - dot(coupling[i, q], picked)
        update[i] = total
        return carry

    lax.fori_loop(0, LEAVES, early_leaf, 0)

    shared[4].wait_recv()
    pltpu.make_async_copy(residual, residual, recv_sem.at[6]).wait()
    for part in range(2):
        for j in range(4 * part, 4 * part + 4):
            late[k, j] = dot(inv2[j], residual[j]).astype(BF16)
        shared.append(share(5 + part, late.at[k, pl.ds(4 * part, 4)]))
    shared[5].wait_recv()
    shared[6].wait_recv()

    def late_leaf(i, carry):
        total = update[i]
        for q in range(EARLY_LINKS, LINKS):
            at = jnp.maximum(links[i, q] - EARLY, 0)
            picked = jnp.concatenate([late[0, at], late[1, at]], axis=1)
            total = total - dot(coupling[i, q], picked)
        leaf_res[i] = dot(inverse[i], total.astype(BF16)).astype(BF16)
        pltpu.make_async_copy(leaf_res.at[i], leaf_out.at[i], out_sem.at[0]).start()
        return carry

    lax.fori_loop(0, LEAVES, late_leaf, 0)

    from_lane = lax.broadcasted_iota(jnp.int32, (HALF, WIDTH), 0)
    to_lane = lax.broadcasted_iota(jnp.int32, (HALF, WIDTH), 1)
    pick = (from_lane == to_lane + WIDTH * slot).astype(F32).astype(BF16)
    mine = early[zhalf, :, rows].reshape(EARLY * ROWS, HALF)
    top_res[pl.ds(0, EARLY)] = dot(mine, pick).astype(BF16).reshape(EARLY, ROWS, WIDTH)
    mine = late[zhalf, :, rows].reshape(LEVEL2 * ROWS, HALF)
    top_res[pl.ds(EARLY, LEVEL2)] = dot(mine, pick).astype(BF16).reshape(LEVEL2, ROWS, WIDTH)
    last = pltpu.make_async_copy(top_res, top_out, out_sem.at[1])
    last.start()

    for copy in shared:
        copy.wait_send()
    others = pl.ds(0, BLOCK - ROWS)
    sent = (
        inv0.at[half0, others],
        coup1.at[pairs, :, others],
        inv1.at[pairs, others],
        inv2.at[pl.ds(4 * k, 4), others],
        zbuf.at[pl.ds(0, DEPTH - 1)],
        sources.at[:, others],
        residual.at[:, others],
    )
    for g, part in enumerate(sent):
        pltpu.make_async_copy(part, part, send_sem.at[g]).wait()

    @pl.when(k != zhalf)
    def _():
        pltpu.make_async_copy(pack, pack, send_sem.at[7]).wait()

    pltpu.make_async_copy(leaf_res, leaf_out, out_sem.at[0]).wait()
    last.wait()


def local(
    top_sources, leaf_sources, top_inverse, leaf_inverse, top_coupling, leaf_coupling, leaf_links
):
    anywhere = pl.BlockSpec(memory_space=pl.ANY)
    vmem, dma = pltpu.VMEM, pltpu.SemaphoreType.DMA
    return pl.pallas_call(
        kernel,
        out_shape=(
            jax.ShapeDtypeStruct((TOP, ROWS, WIDTH), BF16),
            jax.ShapeDtypeStruct((LEAVES, BLOCK, BLOCK), BF16),
        ),
        in_specs=[pl.BlockSpec(memory_space=pltpu.SMEM)] + [anywhere] * 6,
        out_specs=(anywhere, anywhere),
        scratch_shapes=[
            vmem((TOP, ROWS, WIDTH), BF16),
            vmem((ROWS, BLOCK), BF16),
            vmem((DEPTH, ROWS, BLOCK), BF16),
            vmem((TOP, ROWS, HALF), BF16),
            vmem((EARLY, BLOCK, HALF), BF16),
            vmem((LEVEL0, BLOCK, BLOCK), BF16),
            vmem((LEVEL1, BLOCK, BLOCK), BF16),
            vmem((LEVEL2, BLOCK, BLOCK), BF16),
            vmem((LEVEL1, LEVEL0, BLOCK, BLOCK), BF16),
            vmem((LEVEL2, EARLY, ROWS, BLOCK), BF16),
            vmem((2, EARLY, BLOCK, HALF), BF16),
            vmem((2, LEVEL2, BLOCK, HALF), BF16),
            vmem((LEVEL2, ROWS, HALF), BF16),
            vmem((LEVEL2, BLOCK, HALF), BF16),
            vmem((LEAVES, LINKS, BLOCK, BLOCK), BF16),
            vmem((LEAVES, BLOCK, BLOCK), BF16),
            vmem((LEAVES, BLOCK, BLOCK), BF16),
            vmem((LEAVES, BLOCK, BLOCK), F32),
            vmem((LEAVES, BLOCK, BLOCK), BF16),
            vmem((TOP, ROWS, WIDTH), BF16),
            dma((2,)),
            dma((8,)),
            dma((7,)),
            dma((7,)),
            dma((7,)),
            dma((3,)),
            dma((2,)),
        ],
        compiler_params=pltpu.CompilerParams(
            collective_id=0, has_side_effects=True, vmem_limit_bytes=56 * 2**20
        ),
    )(
        leaf_links,
        top_sources,
        leaf_sources,
        top_inverse,
        leaf_inverse,
        top_coupling,
        leaf_coupling,
    )


def solution(mesh):
    in_specs = (
        P(None, "row", "col"),
        P(("col", "row"), None, None),
        P(None, "row", None),
        P(("col", "row"), None, None),
        P(None, None, "row", None),
        P(("col", "row"), None, None, None),
        P(("col", "row"), None),
    )
    out_specs = (P(None, "row", "col"), P(("col", "row"), None, None))
    return jax.shard_map(local, mesh=mesh, in_specs=in_specs, out_specs=out_specs, check_vma=False)
```

```python
import jax
import jax.numpy as jnp
from jax import lax
from jax.experimental import pallas as pl
from jax.experimental.pallas import tpu as pltpu
from jax.sharding import PartitionSpec as P

LEVEL0 = 2
LEVEL1 = 4
LEVEL2 = 8
EARLY = LEVEL0 + LEVEL1
TOP = EARLY + LEVEL2
EARLY_LINKS = 5
LINKS = 9
LEAVES = 8
BLOCK = 256
HALF = 128
ROWS = 16
WIDTH = 16
PLANE = 16
DEPTH = 8
MESH = pl.DeviceIdType.MESH
BF16 = jnp.bfloat16
F32 = jnp.float32


def dot(a, b):
    return jnp.dot(a, b, preferred_element_type=F32)


def kernel(
    links,
    top_sources,
    leaf_sources,
    top_inverse,
    leaf_inverse,
    top_coupling,
    leaf_coupling,
    top_res,
    leaf_res,
    inverse,
    src_own,
    pack,
    picks,
    zbuf,
    src_rows,
    sources,
    inv0,
    inv1,
    inv2,
    coup1,
    coup2,
    early,
    late,
    res_rows,
    residual,
    coupling,
    leaf_src,
    update,
    local_sem,
    send_sem,
    recv_sem,
    core_send,
    core_recv,
    leaf_sem,
):
    col, row = lax.axis_index("col"), lax.axis_index("row")
    z, k = col // 2, lax.rem(col, 2)
    own = pl.multiple_of(row * ROWS, ROWS)
    rows = pl.ds(own, ROWS)
    other = (z * 2 + 1 - k, row)

    def row_peer(d):
        return (col, lax.rem(row + d, PLANE))

    first = pltpu.make_async_copy(top_sources, src_own, local_sem.at[0])
    first.start()
    barrier = pltpu.get_barrier_semaphore()

    def greet(d, carry):
        pl.semaphore_signal(barrier, 1, device_id=row_peer(d), device_id_type=MESH)
        pl.semaphore_signal(
            barrier, 1, device_id=(lax.rem(col + d, PLANE), row), device_id_type=MESH
        )
        return carry

    lax.fori_loop(1, PLANE, greet, 0)
    second = pltpu.make_async_copy(top_coupling.at[pl.ds(LEVEL1, LEVEL2)], coup2, local_sem.at[1])
    second.start()

    half0 = pl.ds(k, 1)
    half1 = pl.ds(LEVEL0 + 2 * k, 2)
    lanes = pl.ds(pl.multiple_of(k * HALF, HALF), HALF)
    pairs = pl.ds(2 * k, 2)
    early_pairs = pl.ds(0, LEVEL0)
    groups = (
        (top_inverse.at[half0], lambda at: inv0.at[half0, at]),
        (
            top_coupling.at[pairs, early_pairs],
            lambda at: coup1.at[pairs, :, at],
        ),
        (top_inverse.at[half1], lambda at: inv1.at[pairs, at]),
        (top_inverse.at[EARLY + z, :, lanes], lambda at: inv2.at[k, z, at]),
    )
    for g, (source, place) in enumerate(groups):
        pltpu.make_async_copy(source, place(rows), recv_sem.at[g]).start()

    first.wait()
    lane = lax.broadcasted_iota(jnp.int32, (WIDTH, BLOCK), 1)
    repeat = (lax.rem(lane, WIDTH) == lax.broadcasted_iota(jnp.int32, (WIDTH, BLOCK), 0)).astype(
        F32
    ).astype(BF16)
    spread = dot(src_own[...].reshape(TOP * ROWS, WIDTH), repeat)
    place_row = lax.broadcasted_iota(jnp.int32, (TOP * ROWS, BLOCK), 0) // ROWS
    place_lane = lax.broadcasted_iota(jnp.int32, (TOP * ROWS, BLOCK), 1) // WIDTH
    spread = jnp.where(place_row == place_lane, spread, 0.0)
    pack[...] = spread.reshape(TOP, ROWS, BLOCK).sum(axis=0).astype(BF16)

    from_lane = lax.broadcasted_iota(jnp.int32, (HALF, HALF), 0)
    to_lane = lax.broadcasted_iota(jnp.int32, (HALF, HALF), 1)
    keep = from_lane // ROWS == to_lane // WIDTH
    for j in range(8):
        picks[j] = (from_lane == lax.rem(to_lane, WIDTH) + WIDTH * j).astype(F32).astype(BF16)

    pl.semaphore_wait(barrier, 2 * (PLANE - 1))

    zhalf = z // 4
    slot = lax.rem(col, 8)

    def send_z(d, carry):
        pltpu.make_async_remote_copy(
            src_ref=pack,
            dst_ref=zbuf.at[slot],
            send_sem=send_sem.at[4],
            recv_sem=recv_sem.at[4],
            device_id=(lax.rem(z + d, DEPTH) * 2 + zhalf, row),
            device_id_type=MESH,
        ).start()
        return carry

    @pl.when(k == zhalf)
    def _():
        pltpu.make_async_copy(pack, zbuf.at[slot], recv_sem.at[4]).start()

    @pl.when(k != zhalf)
    def _():
        pltpu.make_async_remote_copy(
            src_ref=pack,
            dst_ref=zbuf.at[slot],
            send_sem=send_sem.at[7],
            recv_sem=recv_sem.at[4],
            device_id=other,
            device_id_type=MESH,
        ).start()

    lax.fori_loop(1, DEPTH, send_z, 0)

    def gather(g, source, target):
        def send(d, carry):
            pltpu.make_async_remote_copy(
                src_ref=source,
                dst_ref=target,
                send_sem=send_sem.at[g],
                recv_sem=recv_sem.at[g],
                device_id=row_peer(d),
                device_id_type=MESH,
            ).start()
            return carry

        lax.fori_loop(1, PLANE, send, 0)

    for g in (3, 0, 1, 2):
        gather(g, groups[g][0], groups[g][1](rows))

    leaf_copies = (
        pltpu.make_async_copy(leaf_sources, leaf_src, leaf_sem.at[0]),
        pltpu.make_async_copy(leaf_coupling, coupling, leaf_sem.at[1]),
        pltpu.make_async_copy(leaf_inverse, inverse, leaf_sem.at[2]),
    )
    for copy in leaf_copies:
        copy.start()

    pltpu.make_async_copy(zbuf, zbuf, recv_sem.at[4]).wait()
    collected = zbuf[...].reshape(HALF, BLOCK)
    for j in range(TOP):
        moved = dot(collected[:, HALF * (j // 8) : HALF * (j // 8 + 1)], picks[j % 8])
        moved = jnp.where(keep, moved, 0.0).reshape(DEPTH, ROWS, HALF).sum(axis=0).astype(BF16)
        src_rows[j] = moved
    early_rows = src_rows.at[pl.ds(0, EARLY)]
    pltpu.make_async_copy(early_rows, sources.at[:, rows], recv_sem.at[5]).start()
    gather(5, early_rows, sources.at[:, rows])

    mine = inv2.at[k, z]
    pltpu.make_async_copy(mine, mine, recv_sem.at[3]).wait()

    def send_inverse(d, carry):
        pltpu.make_async_remote_copy(
            src_ref=mine,
            dst_ref=mine,
            send_sem=send_sem.at[8],
            recv_sem=recv_sem.at[7],
            device_id=(lax.rem(z + d, DEPTH) * 2 + k, row),
            device_id_type=MESH,
        ).start()
        return carry

    lax.fori_loop(1, DEPTH, send_inverse, 0)
    seven = inv2.at[k, pl.ds(0, DEPTH - 1)]

    halves = (
        inv0.at[half0],
        coup1.at[pairs],
        inv1.at[pairs],
    )

    def share(g, part):
        copy = pltpu.make_async_remote_copy(
            src_ref=part,
            dst_ref=part,
            send_sem=core_send.at[g],
            recv_sem=core_recv.at[g],
            device_id=other,
            device_id_type=MESH,
        )
        copy.start()
        return copy

    shared = []
    for g in range(3):
        pltpu.make_async_copy(halves[g], halves[g], recv_sem.at[g]).wait()
        shared.append(share(g, halves[g]))

    shared[0].wait_recv()
    pltpu.make_async_copy(sources, sources, recv_sem.at[5]).wait()
    for b in range(LEVEL0):
        early[k, b] = dot(inv0[b], sources[b]).astype(BF16)
    shared[1].wait_recv()
    shared[2].wait_recv()
    for j in range(LEVEL1):
        total = dot(
            jnp.concatenate([coup1[j, 0], coup1[j, 1]], axis=1),
            early[k, pl.ds(0, LEVEL0)].reshape(LEVEL0 * BLOCK, HALF),
        )
        rest = (sources[LEVEL0 + j].astype(F32) - total).astype(BF16)
        early[k, LEVEL0 + j] = dot(inv1[j], rest).astype(BF16)

    second.wait()
    wide = [coup2[:, b].reshape(LEVEL2 * ROWS, BLOCK) for b in range(EARLY)]
    total = dot(jnp.concatenate(wide, axis=1), early[k].reshape(EARLY * BLOCK, HALF))
    late_src = src_rows[pl.ds(EARLY, LEVEL2)].astype(F32)
    res_rows[...] = (late_src - total.reshape(LEVEL2, ROWS, HALF)).astype(BF16)
    pltpu.make_async_copy(res_rows, residual.at[:, rows], recv_sem.at[6]).start()
    gather(6, res_rows, residual.at[:, rows])
    shared.append(share(4, early.at[k]))

    shared[3].wait_recv()
    for copy in leaf_copies:
        copy.wait()

    def early_leaf(i, carry):
        wide = jnp.concatenate([coupling[i, q] for q in range(EARLY_LINKS)], axis=1)
        tall = []
        for q in range(EARLY_LINKS):
            at = links[i, q]
            tall.append(jnp.concatenate([early[0, at], early[1, at]], axis=1))
        update[i] = leaf_src[i].astype(F32) - dot(wide, jnp.concatenate(tall, axis=0))
        return carry

    lax.fori_loop(0, LEAVES, early_leaf, 0)
    pltpu.make_async_copy(seven, seven, recv_sem.at[7]).wait()
    shared.append(share(3, inv2.at[k]))

    shared[4].wait_recv()
    pltpu.make_async_copy(residual, residual, recv_sem.at[6]).wait()
    for part in range(2):
        for j in range(4 * part, 4 * part + 4):
            whole = jnp.concatenate([inv2[0, j], inv2[1, j]], axis=1)
            late[k, j] = dot(whole, residual[j]).astype(BF16)
        shared.append(share(5 + part, late.at[k, pl.ds(4 * part, 4)]))
    shared[5].wait_recv()
    shared[6].wait_recv()

    def late_leaf(i, carry):
        wide = jnp.concatenate([coupling[i, q] for q in range(EARLY_LINKS, LINKS)], axis=1)
        tall = []
        for q in range(EARLY_LINKS, LINKS):
            at = jnp.maximum(links[i, q] - EARLY, 0)
            tall.append(jnp.concatenate([late[0, at], late[1, at]], axis=1))
        total = update[i] - dot(wide, jnp.concatenate(tall, axis=0))
        leaf_res[i] = total.astype(BF16)
        return carry

    lax.fori_loop(0, LEAVES, late_leaf, 0, unroll=2)

    from_lane = lax.broadcasted_iota(jnp.int32, (HALF, WIDTH), 0)
    to_lane = lax.broadcasted_iota(jnp.int32, (HALF, WIDTH), 1)
    pick = (from_lane == to_lane + WIDTH * slot).astype(F32).astype(BF16)
    mine = early[zhalf, :, rows].reshape(EARLY * ROWS, HALF)
    top_res[pl.ds(0, EARLY)] = dot(mine, pick).astype(BF16).reshape(EARLY, ROWS, WIDTH)
    mine = late[zhalf, :, rows].reshape(LEVEL2 * ROWS, HALF)
    top_res[pl.ds(EARLY, LEVEL2)] = dot(mine, pick).astype(BF16).reshape(LEVEL2, ROWS, WIDTH)

    for copy in shared:
        copy.wait_send()
    others = pl.ds(0, BLOCK - ROWS)
    sent = (
        inv0.at[half0, others],
        coup1.at[pairs, :, others],
        inv1.at[pairs, others],
        inv2.at[k, z, others],
        zbuf.at[pl.ds(0, DEPTH - 1)],
        sources.at[:, others],
        residual.at[:, others],
    )
    for g, part in enumerate(sent):
        pltpu.make_async_copy(part, part, send_sem.at[g]).wait()

    pltpu.make_async_copy(seven, seven, send_sem.at[8]).wait()

    @pl.when(k != zhalf)
    def _():
        pltpu.make_async_copy(pack, pack, send_sem.at[7]).wait()


def finish(leaf_res, inverse, top_res, top_out, leaf_out, result, sem):
    last = pltpu.make_async_copy(top_res, top_out, sem.at[1])
    last.start()
    for i in range(LEAVES):
        result[i] = dot(inverse[i], leaf_res[i]).astype(BF16)
        pltpu.make_async_copy(result.at[i], leaf_out.at[i], sem.at[0]).start()
    pltpu.make_async_copy(result, leaf_out, sem.at[0]).wait()
    last.wait()


def local(
    top_sources, leaf_sources, top_inverse, leaf_inverse, top_coupling, leaf_coupling, leaf_links
):
    anywhere = pl.BlockSpec(memory_space=pltpu.HBM)
    vmem, dma = pltpu.VMEM, pltpu.SemaphoreType.DMA
    held = pl.BlockSpec(memory_space=vmem)
    top_res, leaf_res, inverse = pl.pallas_call(
        kernel,
        out_shape=(
            vmem((TOP, ROWS, WIDTH), BF16),
            vmem((LEAVES, BLOCK, BLOCK), BF16),
            vmem((LEAVES, BLOCK, BLOCK), BF16),
        ),
        in_specs=[pl.BlockSpec(memory_space=pltpu.SMEM)] + [anywhere] * 6,
        out_specs=(held, held, held),
        scratch_shapes=[
            vmem((TOP, ROWS, WIDTH), BF16),
            vmem((ROWS, BLOCK), BF16),
            vmem((8, HALF, HALF), BF16),
            vmem((DEPTH, ROWS, BLOCK), BF16),
            vmem((TOP, ROWS, HALF), BF16),
            vmem((EARLY, BLOCK, HALF), BF16),
            vmem((LEVEL0, BLOCK, BLOCK), BF16),
            vmem((LEVEL1, BLOCK, BLOCK), BF16),
            vmem((2, LEVEL2, BLOCK, HALF), BF16),
            vmem((LEVEL1, LEVEL0, BLOCK, BLOCK), BF16),
            vmem((LEVEL2, EARLY, ROWS, BLOCK), BF16),
            vmem((2, EARLY, BLOCK, HALF), BF16),
            vmem((2, LEVEL2, BLOCK, HALF), BF16),
            vmem((LEVEL2, ROWS, HALF), BF16),
            vmem((LEVEL2, BLOCK, HALF), BF16),
            vmem((LEAVES, LINKS, BLOCK, BLOCK), BF16),
            vmem((LEAVES, BLOCK, BLOCK), BF16),
            vmem((LEAVES, BLOCK, BLOCK), F32),
            dma((2,)),
            dma((9,)),
            dma((8,)),
            dma((7,)),
            dma((7,)),
            dma((3,)),
        ],
        compiler_params=pltpu.CompilerParams(
            collective_id=0, has_side_effects=True, vmem_limit_bytes=59 * 2**20
        ),
    )(
        leaf_links,
        top_sources,
        leaf_sources,
        top_inverse,
        leaf_inverse,
        top_coupling,
        leaf_coupling,
    )
    return pl.pallas_call(
        finish,
        out_shape=(
            jax.ShapeDtypeStruct((TOP, ROWS, WIDTH), BF16),
            jax.ShapeDtypeStruct((LEAVES, BLOCK, BLOCK), BF16),
        ),
        in_specs=[held] * 3,
        out_specs=(anywhere, anywhere),
        scratch_shapes=[vmem((LEAVES, BLOCK, BLOCK), BF16), dma((2,))],
        compiler_params=pltpu.CompilerParams(vmem_limit_bytes=16 * 2**20),
    )(leaf_res, inverse, top_res)


def solution(mesh):
    in_specs = (
        P(None, "row", "col"),
        P(("col", "row"), None, None),
        P(None, "row", None),
        P(("col", "row"), None, None),
        P(None, None, "row", None),
        P(("col", "row"), None, None, None),
        P(("col", "row"), None),
    )
    out_specs = (P(None, "row", "col"), P(("col", "row"), None, None))
    return jax.shard_map(local, mesh=mesh, in_specs=in_specs, out_specs=out_specs, check_vma=False)
```

```python
import jax
import jax.numpy as jnp
from jax import lax
from jax.experimental import pallas as pl
from jax.experimental.pallas import tpu as pltpu
from jax.sharding import PartitionSpec as P

LEVEL0 = 2
LEVEL1 = 4
LEVEL2 = 8
EARLY = LEVEL0 + LEVEL1
TOP = EARLY + LEVEL2
EARLY_LINKS = 5
LINKS = 9
LEAVES = 8
BLOCK = 256
HALF = 128
ROWS = 16
WIDTH = 16
PLANE = 16
SIDE = 4
DEPTH = 8
MESH = pl.DeviceIdType.MESH
BF16 = jnp.bfloat16
F32 = jnp.float32


def dot(a, b):
    return jnp.dot(a, b, preferred_element_type=F32)


def kernel(
    links,
    top_sources,
    leaf_sources,
    top_inverse,
    leaf_inverse,
    top_coupling,
    leaf_coupling,
    top_res,
    leaf_res,
    inverse,
    src_own,
    pack,
    picks,
    zbuf,
    src_rows,
    sources,
    inv0,
    inv1,
    inv2,
    coup1,
    coup2,
    early,
    late,
    res_rows,
    residual,
    coupling,
    leaf_src,
    update,
    local_sem,
    send_sem,
    recv_sem,
    core_send,
    core_recv,
    leaf_sem,
):
    col, row = lax.axis_index("col"), lax.axis_index("row")
    z, k = col // 2, lax.rem(col, 2)
    own = pl.multiple_of(row * ROWS, ROWS)
    rows = pl.ds(own, ROWS)
    other = (z * 2 + 1 - k, row)
    x, y = row // SIDE, lax.rem(row, SIDE)

    def row_peer(d):
        return (col, lax.rem(row + d, PLANE))

    first = pltpu.make_async_copy(top_sources, src_own, local_sem.at[0])
    first.start()
    barrier = pltpu.get_barrier_semaphore()

    def greet(d, carry):
        pl.semaphore_signal(barrier, 1, device_id=row_peer(d), device_id_type=MESH)
        pl.semaphore_signal(
            barrier, 1, device_id=(lax.rem(col + d, PLANE), row), device_id_type=MESH
        )
        return carry

    lax.fori_loop(1, PLANE, greet, 0)
    second = pltpu.make_async_copy(top_coupling.at[pl.ds(LEVEL1, LEVEL2)], coup2, local_sem.at[1])
    second.start()

    half0 = pl.ds(k, 1)
    half1 = pl.ds(LEVEL0 + 2 * k, 2)
    lanes = pl.ds(pl.multiple_of(k * HALF, HALF), HALF)
    pairs = pl.ds(2 * k, 2)
    early_pairs = pl.ds(0, LEVEL0)
    groups = (
        (top_inverse.at[half0], lambda at: inv0.at[half0, at]),
        (
            top_coupling.at[pairs, early_pairs],
            lambda at: coup1.at[pairs, :, x, y],
        ),
        (top_inverse.at[half1], lambda at: inv1.at[pairs, at]),
        (top_inverse.at[EARLY + z, :, lanes], lambda at: inv2.at[k, z, at]),
    )
    for g, (source, place) in enumerate(groups):
        pltpu.make_async_copy(source, place(rows), recv_sem.at[g]).start()

    first.wait()
    lane = lax.broadcasted_iota(jnp.int32, (WIDTH, BLOCK), 1)
    repeat = (lax.rem(lane, WIDTH) == lax.broadcasted_iota(jnp.int32, (WIDTH, BLOCK), 0)).astype(
        F32
    ).astype(BF16)
    spread = dot(src_own[...].reshape(TOP * ROWS, WIDTH), repeat)
    place_row = lax.broadcasted_iota(jnp.int32, (TOP * ROWS, BLOCK), 0) // ROWS
    place_lane = lax.broadcasted_iota(jnp.int32, (TOP * ROWS, BLOCK), 1) // WIDTH
    spread = jnp.where(place_row == place_lane, spread, 0.0)
    pack[...] = spread.reshape(TOP, ROWS, BLOCK).sum(axis=0).astype(BF16)

    from_lane = lax.broadcasted_iota(jnp.int32, (HALF, HALF), 0)
    to_lane = lax.broadcasted_iota(jnp.int32, (HALF, HALF), 1)
    keep = from_lane // ROWS == to_lane // WIDTH
    for j in range(8):
        picks[j] = (from_lane == lax.rem(to_lane, WIDTH) + WIDTH * j).astype(F32).astype(BF16)

    pl.semaphore_wait(barrier, 2 * (PLANE - 1))

    zhalf = z // 4
    slot = lax.rem(col, 8)

    def send_z(d, carry):
        pltpu.make_async_remote_copy(
            src_ref=pack,
            dst_ref=zbuf.at[slot],
            send_sem=send_sem.at[4],
            recv_sem=recv_sem.at[4],
            device_id=(lax.rem(z + d, DEPTH) * 2 + zhalf, row),
            device_id_type=MESH,
        ).start()
        return carry

    @pl.when(k == zhalf)
    def _():
        pltpu.make_async_copy(pack, zbuf.at[slot], recv_sem.at[4]).start()

    @pl.when(k != zhalf)
    def _():
        pltpu.make_async_remote_copy(
            src_ref=pack,
            dst_ref=zbuf.at[slot],
            send_sem=send_sem.at[7],
            recv_sem=recv_sem.at[4],
            device_id=other,
            device_id_type=MESH,
        ).start()

    lax.fori_loop(1, DEPTH, send_z, 0)

    def gather_weights(g, source, target):
        def send(d, carry):
            pltpu.make_async_remote_copy(
                src_ref=source,
                dst_ref=target,
                send_sem=send_sem.at[g],
                recv_sem=recv_sem.at[g],
                device_id=row_peer(d),
                device_id_type=MESH,
            ).start()
            return carry

        lax.fori_loop(1, PLANE, send, 0)

    def along(axis, g, r, source, target):
        def send(d, carry):
            peer = lax.rem(x + d, SIDE) * SIDE + y if axis == 0 else x * SIDE + lax.rem(y + d, SIDE)
            pltpu.make_async_remote_copy(
                src_ref=source,
                dst_ref=target,
                send_sem=send_sem.at[g],
                recv_sem=recv_sem.at[r],
                device_id=(col, peer),
                device_id_type=MESH,
            ).start()
            return carry

        lax.fori_loop(1, SIDE, send, 0)

    for core in range(2):

        @pl.when(k == core)
        def _(core=core):
            along(1 - core, 1, 1, groups[1][0], groups[1][1](rows))

    for g in (3, 0, 2):
        gather_weights(g, groups[g][0], groups[g][1](rows))

    leaf_copies = (
        pltpu.make_async_copy(leaf_sources, leaf_src, leaf_sem.at[0]),
        pltpu.make_async_copy(leaf_coupling, coupling, leaf_sem.at[1]),
        pltpu.make_async_copy(leaf_inverse, inverse, leaf_sem.at[2]),
    )
    for copy in leaf_copies:
        copy.start()

    for core in range(2):

        @pl.when(k == core)
        def _(core=core):
            line = coup1.at[pairs, :, x] if core == 0 else coup1.at[pairs, :, :, y]
            pltpu.make_async_copy(line, line, recv_sem.at[1]).wait()
            along(core, 9, 8, line, line)

    pltpu.make_async_copy(zbuf, zbuf, recv_sem.at[4]).wait()

    def unpack(start, stop):
        collected = zbuf[...].reshape(HALF, BLOCK)
        for j in range(start, stop):
            moved = dot(collected[:, HALF * (j // 8) : HALF * (j // 8 + 1)], picks[j % 8])
            moved = jnp.where(keep, moved, 0.0).reshape(DEPTH, ROWS, HALF).sum(axis=0)
            src_rows[j] = moved.astype(BF16)

    def gather(g, r, source, target):
        pltpu.make_async_copy(source, target(rows), recv_sem.at[r]).start()

        def send(d, carry):
            pltpu.make_async_remote_copy(
                src_ref=source,
                dst_ref=target(rows),
                send_sem=send_sem.at[g],
                recv_sem=recv_sem.at[r],
                device_id=row_peer(d),
                device_id_type=MESH,
            ).start()
            return carry

        lax.fori_loop(1, PLANE, send, 0)

    level0, level1 = pl.ds(0, LEVEL0), pl.ds(LEVEL0, LEVEL1)
    unpack(0, LEVEL0)
    gather(5, 5, src_rows.at[level0], lambda at: sources.at[level0, at])
    unpack(LEVEL0, EARLY)
    gather(10, 9, src_rows.at[level1], lambda at: sources.at[level1, at])

    mine = inv2.at[k, z]
    pltpu.make_async_copy(mine, mine, recv_sem.at[3]).wait()

    def send_inverse(d, carry):
        pltpu.make_async_remote_copy(
            src_ref=mine,
            dst_ref=mine,
            send_sem=send_sem.at[8],
            recv_sem=recv_sem.at[7],
            device_id=(lax.rem(z + d, DEPTH) * 2 + k, row),
            device_id_type=MESH,
        ).start()
        return carry

    lax.fori_loop(1, DEPTH, send_inverse, 0)
    seven = inv2.at[k, pl.ds(0, DEPTH - 1)]
    unpack(EARLY, TOP)

    halves = (
        inv0.at[half0],
        coup1.at[pairs],
        inv1.at[pairs],
    )

    def share(g, part):
        copy = pltpu.make_async_remote_copy(
            src_ref=part,
            dst_ref=part,
            send_sem=core_send.at[g],
            recv_sem=core_recv.at[g],
            device_id=other,
            device_id_type=MESH,
        )
        copy.start()
        return copy

    shared = []
    three = coup1.at[pairs, :, pl.ds(0, SIDE - 1)]
    for g, r, part in ((0, 0, halves[0]), (1, 8, three), (2, 2, halves[2])):
        pltpu.make_async_copy(part, part, recv_sem.at[r]).wait()
        shared.append(share(g, halves[g]))

    shared[0].wait_recv()
    part = sources.at[level0]
    pltpu.make_async_copy(part, part, recv_sem.at[5]).wait()
    for b in range(LEVEL0):
        early[k, b] = dot(inv0[b], sources[b]).astype(BF16)
    shared[1].wait_recv()
    totals = []
    for j in range(LEVEL1):
        wide = [coup1[j, b].reshape(BLOCK, BLOCK) for b in range(LEVEL0)]
        tall = early[k, pl.ds(0, LEVEL0)].reshape(LEVEL0 * BLOCK, HALF)
        totals.append(dot(jnp.concatenate(wide, axis=1), tall))
    shared[2].wait_recv()
    part = sources.at[level1]
    pltpu.make_async_copy(part, part, recv_sem.at[9]).wait()
    for j in range(LEVEL1):
        rest = (sources[LEVEL0 + j].astype(F32) - totals[j]).astype(BF16)
        early[k, LEVEL0 + j] = dot(inv1[j], rest).astype(BF16)

    second.wait()
    wide = [coup2[:, b].reshape(LEVEL2 * ROWS, BLOCK) for b in range(EARLY)]
    total = dot(jnp.concatenate(wide, axis=1), early[k].reshape(EARLY * BLOCK, HALF))
    late_src = src_rows[pl.ds(EARLY, LEVEL2)].astype(F32)
    res_rows[...] = (late_src - total.reshape(LEVEL2, ROWS, HALF)).astype(BF16)
    chunks = (pl.ds(0, 4), pl.ds(4, 4))
    for part, (g, r) in enumerate(((6, 6), (11, 10))):
        chunk = chunks[part]
        gather(g, r, res_rows.at[chunk], lambda at, chunk=chunk: residual.at[chunk, at])
    shared.append(share(4, early.at[k]))

    shared[3].wait_recv()

    from_lane = lax.broadcasted_iota(jnp.int32, (HALF, WIDTH), 0)
    to_lane = lax.broadcasted_iota(jnp.int32, (HALF, WIDTH), 1)
    pick = (from_lane == to_lane + WIDTH * slot).astype(F32).astype(BF16)
    first_rows = early[zhalf, :, rows].reshape(EARLY * ROWS, HALF)
    top_res[pl.ds(0, EARLY)] = dot(first_rows, pick).astype(BF16).reshape(EARLY, ROWS, WIDTH)
    for copy in leaf_copies:
        copy.wait()

    def early_leaf(i, carry):
        wide = jnp.concatenate([coupling[i, q] for q in range(EARLY_LINKS)], axis=1)
        tall = []
        for q in range(EARLY_LINKS):
            at = links[i, q]
            tall.append(jnp.concatenate([early[0, at], early[1, at]], axis=1))
        update[i] = leaf_src[i].astype(F32) - dot(wide, jnp.concatenate(tall, axis=0))
        return carry

    lax.fori_loop(0, LEAVES, early_leaf, 0)
    pltpu.make_async_copy(seven, seven, recv_sem.at[7]).wait()
    shared.append(share(3, inv2.at[k]))

    shared[4].wait_recv()
    for part in range(2):
        chunk = residual.at[chunks[part]]
        pltpu.make_async_copy(chunk, chunk, recv_sem.at[(6, 10)[part]]).wait()
        for j in range(4 * part, 4 * part + 4):
            whole = jnp.concatenate([inv2[0, j], inv2[1, j]], axis=1)
            late[k, j] = dot(whole, residual[j]).astype(BF16)
        shared.append(share(5 + part, late.at[k, pl.ds(4 * part, 4)]))
    shared[5].wait_recv()
    shared[6].wait_recv()

    def late_leaf(i, carry):
        wide = jnp.concatenate([coupling[i, q] for q in range(EARLY_LINKS, LINKS)], axis=1)
        tall = []
        for q in range(EARLY_LINKS, LINKS):
            at = jnp.maximum(links[i, q] - EARLY, 0)
            tall.append(jnp.concatenate([late[0, at], late[1, at]], axis=1))
        total = update[i] - dot(wide, jnp.concatenate(tall, axis=0))
        leaf_res[i] = total.astype(BF16)
        return carry

    lax.fori_loop(0, LEAVES, late_leaf, 0, unroll=2)

    rest = late[zhalf, :, rows].reshape(LEVEL2 * ROWS, HALF)
    top_res[pl.ds(EARLY, LEVEL2)] = dot(rest, pick).astype(BF16).reshape(LEVEL2, ROWS, WIDTH)

    for copy in shared:
        copy.wait_send()
    others = pl.ds(0, BLOCK - ROWS)
    sent = (
        (0, inv0.at[half0, others]),
        (1, coup1.at[pairs, :, 0, pl.ds(0, SIDE - 1)]),
        (2, inv1.at[pairs, others]),
        (3, inv2.at[k, z, others]),
        (4, zbuf.at[pl.ds(0, DEPTH - 1)]),
        (5, sources.at[level0, others]),
        (6, residual.at[chunks[0], others]),
        (9, three),
        (10, sources.at[level1, others]),
        (11, residual.at[chunks[1], others]),
    )
    for g, part in sent:
        pltpu.make_async_copy(part, part, send_sem.at[g]).wait()

    pltpu.make_async_copy(seven, seven, send_sem.at[8]).wait()

    @pl.when(k != zhalf)
    def _():
        pltpu.make_async_copy(pack, pack, send_sem.at[7]).wait()


def finish(leaf_res, inverse, top_res, top_out, leaf_out, result, sem):
    last = pltpu.make_async_copy(top_res, top_out, sem.at[1])
    last.start()
    for i in range(LEAVES):
        result[i] = dot(inverse[i], leaf_res[i]).astype(BF16)
        pltpu.make_async_copy(result.at[i], leaf_out.at[i], sem.at[0]).start()
    pltpu.make_async_copy(result, leaf_out, sem.at[0]).wait()
    last.wait()


def local(
    top_sources, leaf_sources, top_inverse, leaf_inverse, top_coupling, leaf_coupling, leaf_links
):
    anywhere = pl.BlockSpec(memory_space=pltpu.HBM)
    vmem, dma = pltpu.VMEM, pltpu.SemaphoreType.DMA
    held = pl.BlockSpec(memory_space=vmem)
    top_res, leaf_res, inverse = pl.pallas_call(
        kernel,
        out_shape=(
            vmem((TOP, ROWS, WIDTH), BF16),
            vmem((LEAVES, BLOCK, BLOCK), BF16),
            vmem((LEAVES, BLOCK, BLOCK), BF16),
        ),
        in_specs=[pl.BlockSpec(memory_space=pltpu.SMEM)] + [anywhere] * 6,
        out_specs=(held, held, held),
        scratch_shapes=[
            vmem((TOP, ROWS, WIDTH), BF16),
            vmem((ROWS, BLOCK), BF16),
            vmem((8, HALF, HALF), BF16),
            vmem((DEPTH, ROWS, BLOCK), BF16),
            vmem((TOP, ROWS, HALF), BF16),
            vmem((EARLY, BLOCK, HALF), BF16),
            vmem((LEVEL0, BLOCK, BLOCK), BF16),
            vmem((LEVEL1, BLOCK, BLOCK), BF16),
            vmem((2, LEVEL2, BLOCK, HALF), BF16),
            vmem((LEVEL1, LEVEL0, SIDE, SIDE, ROWS, BLOCK), BF16),
            vmem((LEVEL2, EARLY, ROWS, BLOCK), BF16),
            vmem((2, EARLY, BLOCK, HALF), BF16),
            vmem((2, LEVEL2, BLOCK, HALF), BF16),
            vmem((LEVEL2, ROWS, HALF), BF16),
            vmem((LEVEL2, BLOCK, HALF), BF16),
            vmem((LEAVES, LINKS, BLOCK, BLOCK), BF16),
            vmem((LEAVES, BLOCK, BLOCK), BF16),
            vmem((LEAVES, BLOCK, BLOCK), F32),
            dma((2,)),
            dma((12,)),
            dma((11,)),
            dma((7,)),
            dma((7,)),
            dma((3,)),
        ],
        compiler_params=pltpu.CompilerParams(
            collective_id=0, has_side_effects=True, vmem_limit_bytes=59 * 2**20
        ),
    )(
        leaf_links,
        top_sources,
        leaf_sources,
        top_inverse,
        leaf_inverse,
        top_coupling,
        leaf_coupling,
    )
    return pl.pallas_call(
        finish,
        out_shape=(
            jax.ShapeDtypeStruct((TOP, ROWS, WIDTH), BF16),
            jax.ShapeDtypeStruct((LEAVES, BLOCK, BLOCK), BF16),
        ),
        in_specs=[held] * 3,
        out_specs=(anywhere, anywhere),
        scratch_shapes=[vmem((LEAVES, BLOCK, BLOCK), BF16), dma((2,))],
        compiler_params=pltpu.CompilerParams(vmem_limit_bytes=16 * 2**20),
    )(leaf_res, inverse, top_res)


def solution(mesh):
    in_specs = (
        P(None, "row", "col"),
        P(("col", "row"), None, None),
        P(None, "row", None),
        P(("col", "row"), None, None),
        P(None, None, "row", None),
        P(("col", "row"), None, None, None),
        P(("col", "row"), None),
    )
    out_specs = (P(None, "row", "col"), P(("col", "row"), None, None))
    return jax.shard_map(local, mesh=mesh, in_specs=in_specs, out_specs=out_specs, check_vma=False)
```

```python
import jax
import jax.numpy as jnp
from jax import lax
from jax.experimental import pallas as pl
from jax.experimental.pallas import tpu as pltpu
from jax.sharding import PartitionSpec as P

LEVEL0 = 2
LEVEL1 = 4
LEVEL2 = 8
EARLY = LEVEL0 + LEVEL1
TOP = EARLY + LEVEL2
EARLY_LINKS = 5
LINKS = 9
LEAVES = 8
BLOCK = 256
HALF = 128
ROWS = 16
WIDTH = 16
PLANE = 16
SIDE = 4
DEPTH = 8
MESH = pl.DeviceIdType.MESH
BF16 = jnp.bfloat16
F32 = jnp.float32


def dot(a, b):
    return jnp.dot(a, b, preferred_element_type=F32)


def kernel(
    links,
    top_sources,
    leaf_sources,
    top_inverse,
    leaf_inverse,
    top_coupling,
    leaf_coupling,
    top_res,
    leaf_res,
    inverse,
    src_own,
    pack,
    picks,
    zbuf,
    src_rows,
    sources,
    inv0,
    inv1,
    inv2,
    coup1,
    coup2,
    early,
    late,
    res_rows,
    residual,
    coupling,
    leaf_src,
    update,
    local_sem,
    send_sem,
    recv_sem,
    core_send,
    core_recv,
    leaf_sem,
):
    col, row = lax.axis_index("col"), lax.axis_index("row")
    z, k = col // 2, lax.rem(col, 2)
    own = pl.multiple_of(row * ROWS, ROWS)
    rows = pl.ds(own, ROWS)
    other = (z * 2 + 1 - k, row)
    x, y = row // SIDE, lax.rem(row, SIDE)

    def row_peer(d):
        return (col, lax.rem(row + d, PLANE))

    first = pltpu.make_async_copy(top_sources, src_own, local_sem.at[0])
    first.start()
    barrier = pltpu.get_barrier_semaphore()

    def greet(d, carry):
        pl.semaphore_signal(barrier, 1, device_id=row_peer(d), device_id_type=MESH)
        pl.semaphore_signal(
            barrier, 1, device_id=(lax.rem(col + d, PLANE), row), device_id_type=MESH
        )
        return carry

    lax.fori_loop(1, PLANE, greet, 0)
    second = pltpu.make_async_copy(top_coupling.at[pl.ds(LEVEL1, LEVEL2)], coup2, local_sem.at[1])
    second.start()

    half0 = pl.ds(k, 1)
    half1 = pl.ds(LEVEL0 + 2 * k, 2)
    lanes = pl.ds(pl.multiple_of(k * HALF, HALF), HALF)
    pairs = pl.ds(2 * k, 2)
    early_pairs = pl.ds(0, LEVEL0)
    groups = (
        (top_inverse.at[half0], lambda at: inv0.at[half0, at]),
        (
            top_coupling.at[pairs, early_pairs],
            lambda at: coup1.at[pairs, :, x, y],
        ),
        (top_inverse.at[half1], lambda at: inv1.at[pairs, x, y]),
        (top_inverse.at[EARLY + z, :, lanes], lambda at: inv2.at[k, z, at]),
    )
    for g, (source, place) in enumerate(groups):
        pltpu.make_async_copy(source, place(rows), recv_sem.at[g]).start()

    first.wait()
    lane = lax.broadcasted_iota(jnp.int32, (WIDTH, BLOCK), 1)
    repeat = (lax.rem(lane, WIDTH) == lax.broadcasted_iota(jnp.int32, (WIDTH, BLOCK), 0)).astype(
        F32
    ).astype(BF16)
    spread = dot(src_own[...].reshape(TOP * ROWS, WIDTH), repeat)
    place_row = lax.broadcasted_iota(jnp.int32, (TOP * ROWS, BLOCK), 0) // ROWS
    place_lane = lax.broadcasted_iota(jnp.int32, (TOP * ROWS, BLOCK), 1) // WIDTH
    spread = jnp.where(place_row == place_lane, spread, 0.0)
    pack[...] = spread.reshape(TOP, ROWS, BLOCK).sum(axis=0).astype(BF16)

    from_lane = lax.broadcasted_iota(jnp.int32, (HALF, HALF), 0)
    to_lane = lax.broadcasted_iota(jnp.int32, (HALF, HALF), 1)
    keep = from_lane // ROWS == to_lane // WIDTH
    for j in range(8):
        picks[j] = (from_lane == lax.rem(to_lane, WIDTH) + WIDTH * j).astype(F32).astype(BF16)

    pl.semaphore_wait(barrier, 2 * (PLANE - 1))

    zhalf = z // 4
    slot = lax.rem(col, 8)

    def send_z(d, carry):
        pltpu.make_async_remote_copy(
            src_ref=pack,
            dst_ref=zbuf.at[slot],
            send_sem=send_sem.at[4],
            recv_sem=recv_sem.at[4],
            device_id=(lax.rem(z + d, DEPTH) * 2 + zhalf, row),
            device_id_type=MESH,
        ).start()
        return carry

    @pl.when(k == zhalf)
    def _():
        pltpu.make_async_copy(pack, zbuf.at[slot], recv_sem.at[4]).start()

    @pl.when(k != zhalf)
    def _():
        pltpu.make_async_remote_copy(
            src_ref=pack,
            dst_ref=zbuf.at[slot],
            send_sem=send_sem.at[7],
            recv_sem=recv_sem.at[4],
            device_id=other,
            device_id_type=MESH,
        ).start()

    lax.fori_loop(1, DEPTH, send_z, 0)

    def gather_weights(g, source, target):
        def send(d, carry):
            pltpu.make_async_remote_copy(
                src_ref=source,
                dst_ref=target,
                send_sem=send_sem.at[g],
                recv_sem=recv_sem.at[g],
                device_id=row_peer(d),
                device_id_type=MESH,
            ).start()
            return carry

        lax.fori_loop(1, PLANE, send, 0)

    def along(axis, g, r, source, target):
        def send(d, carry):
            peer = lax.rem(x + d, SIDE) * SIDE + y if axis == 0 else x * SIDE + lax.rem(y + d, SIDE)
            pltpu.make_async_remote_copy(
                src_ref=source,
                dst_ref=target,
                send_sem=send_sem.at[g],
                recv_sem=recv_sem.at[r],
                device_id=(col, peer),
                device_id_type=MESH,
            ).start()
            return carry

        lax.fori_loop(1, SIDE, send, 0)

    for core in range(2):

        @pl.when(k == core)
        def _(core=core):
            along(1 - core, 1, 1, groups[1][0], groups[1][1](rows))
            along(1 - core, 2, 2, groups[2][0], groups[2][1](rows))

    for g in (3, 0):
        gather_weights(g, groups[g][0], groups[g][1](rows))

    leaf_copies = (
        pltpu.make_async_copy(leaf_sources, leaf_src, leaf_sem.at[0]),
        pltpu.make_async_copy(leaf_coupling, coupling, leaf_sem.at[1]),
        pltpu.make_async_copy(leaf_inverse, inverse, leaf_sem.at[2]),
    )
    for copy in leaf_copies:
        copy.start()

    for core in range(2):

        @pl.when(k == core)
        def _(core=core):
            line = coup1.at[pairs, :, x] if core == 0 else coup1.at[pairs, :, :, y]
            pltpu.make_async_copy(line, line, recv_sem.at[1]).wait()
            along(core, 9, 8, line, line)
            line = inv1.at[pairs, x] if core == 0 else inv1.at[pairs, :, y]
            pltpu.make_async_copy(line, line, recv_sem.at[2]).wait()
            along(core, 12, 11, line, line)

    pltpu.make_async_copy(zbuf, zbuf, recv_sem.at[4]).wait()

    def unpack(start, stop):
        collected = zbuf[...].reshape(HALF, BLOCK)
        for j in range(start, stop):
            moved = dot(collected[:, HALF * (j // 8) : HALF * (j // 8 + 1)], picks[j % 8])
            moved = jnp.where(keep, moved, 0.0).reshape(DEPTH, ROWS, HALF).sum(axis=0)
            src_rows[j] = moved.astype(BF16)

    def gather(g, r, source, target):
        pltpu.make_async_copy(source, target(rows), recv_sem.at[r]).start()

        def send(d, carry):
            pltpu.make_async_remote_copy(
                src_ref=source,
                dst_ref=target(rows),
                send_sem=send_sem.at[g],
                recv_sem=recv_sem.at[r],
                device_id=row_peer(d),
                device_id_type=MESH,
            ).start()
            return carry

        lax.fori_loop(1, PLANE, send, 0)

    level0, level1 = pl.ds(0, LEVEL0), pl.ds(LEVEL0, LEVEL1)
    unpack(0, LEVEL0)
    gather(5, 5, src_rows.at[level0], lambda at: sources.at[level0, at])
    unpack(LEVEL0, EARLY)
    gather(10, 9, src_rows.at[level1], lambda at: sources.at[level1, at])

    mine = inv2.at[k, z]
    pltpu.make_async_copy(mine, mine, recv_sem.at[3]).wait()

    def send_inverse(d, carry):
        pltpu.make_async_remote_copy(
            src_ref=mine,
            dst_ref=mine,
            send_sem=send_sem.at[8],
            recv_sem=recv_sem.at[7],
            device_id=(lax.rem(z + d, DEPTH) * 2 + k, row),
            device_id_type=MESH,
        ).start()
        return carry

    lax.fori_loop(1, DEPTH, send_inverse, 0)
    seven = inv2.at[k, pl.ds(0, DEPTH - 1)]
    unpack(EARLY, TOP)

    halves = (
        inv0.at[half0],
        coup1.at[pairs],
        inv1.at[pairs],
    )

    def share(g, part):
        copy = pltpu.make_async_remote_copy(
            src_ref=part,
            dst_ref=part,
            send_sem=core_send.at[g],
            recv_sem=core_recv.at[g],
            device_id=other,
            device_id_type=MESH,
        )
        copy.start()
        return copy

    shared = []
    three = coup1.at[pairs, :, pl.ds(0, SIDE - 1)]
    three_inv = inv1.at[pairs, pl.ds(0, SIDE - 1)]
    for g, r, part in ((0, 0, halves[0]), (1, 8, three), (2, 11, three_inv)):
        pltpu.make_async_copy(part, part, recv_sem.at[r]).wait()
        shared.append(share(g, halves[g]))

    shared[0].wait_recv()
    part = sources.at[level0]
    pltpu.make_async_copy(part, part, recv_sem.at[5]).wait()
    for b in range(LEVEL0):
        early[k, b] = dot(inv0[b], sources[b]).astype(BF16)
    shared[1].wait_recv()
    totals = []
    for j in range(LEVEL1):
        wide = [coup1[j, b].reshape(BLOCK, BLOCK) for b in range(LEVEL0)]
        tall = early[k, pl.ds(0, LEVEL0)].reshape(LEVEL0 * BLOCK, HALF)
        totals.append(dot(jnp.concatenate(wide, axis=1), tall))
    shared[2].wait_recv()
    part = sources.at[level1]
    pltpu.make_async_copy(part, part, recv_sem.at[9]).wait()
    for j in range(LEVEL1):
        rest = (sources[LEVEL0 + j].astype(F32) - totals[j]).astype(BF16)
        early[k, LEVEL0 + j] = dot(inv1[j].reshape(BLOCK, BLOCK), rest).astype(BF16)

    second.wait()
    wide = [coup2[:, b].reshape(LEVEL2 * ROWS, BLOCK) for b in range(EARLY)]
    total = dot(jnp.concatenate(wide, axis=1), early[k].reshape(EARLY * BLOCK, HALF))
    late_src = src_rows[pl.ds(EARLY, LEVEL2)].astype(F32)
    res_rows[...] = (late_src - total.reshape(LEVEL2, ROWS, HALF)).astype(BF16)
    chunks = (pl.ds(0, 4), pl.ds(4, 4))
    for part, (g, r) in enumerate(((6, 6), (11, 10))):
        chunk = chunks[part]
        gather(g, r, res_rows.at[chunk], lambda at, chunk=chunk: residual.at[chunk, at])
    shared.append(share(4, early.at[k]))

    shared[3].wait_recv()

    from_lane = lax.broadcasted_iota(jnp.int32, (HALF, WIDTH), 0)
    to_lane = lax.broadcasted_iota(jnp.int32, (HALF, WIDTH), 1)
    pick = (from_lane == to_lane + WIDTH * slot).astype(F32).astype(BF16)
    first_rows = early[zhalf, :, rows].reshape(EARLY * ROWS, HALF)
    top_res[pl.ds(0, EARLY)] = dot(first_rows, pick).astype(BF16).reshape(EARLY, ROWS, WIDTH)
    for copy in leaf_copies:
        copy.wait()

    def early_leaf(i, carry):
        wide = jnp.concatenate([coupling[i, q] for q in range(EARLY_LINKS)], axis=1)
        tall = []
        for q in range(EARLY_LINKS):
            at = links[i, q]
            tall.append(jnp.concatenate([early[0, at], early[1, at]], axis=1))
        update[i] = leaf_src[i].astype(F32) - dot(wide, jnp.concatenate(tall, axis=0))
        return carry

    lax.fori_loop(0, LEAVES, early_leaf, 0)
    pltpu.make_async_copy(seven, seven, recv_sem.at[7]).wait()
    shared.append(share(3, inv2.at[k]))

    shared[4].wait_recv()
    for part in range(2):
        chunk = residual.at[chunks[part]]
        pltpu.make_async_copy(chunk, chunk, recv_sem.at[(6, 10)[part]]).wait()
        for j in range(4 * part, 4 * part + 4):
            whole = jnp.concatenate([inv2[0, j], inv2[1, j]], axis=1)
            late[k, j] = dot(whole, residual[j]).astype(BF16)
        shared.append(share(5 + part, late.at[k, pl.ds(4 * part, 4)]))
    shared[5].wait_recv()
    shared[6].wait_recv()

    def late_leaf(i, carry):
        wide = jnp.concatenate([coupling[i, q] for q in range(EARLY_LINKS, LINKS)], axis=1)
        tall = []
        for q in range(EARLY_LINKS, LINKS):
            at = jnp.maximum(links[i, q] - EARLY, 0)
            tall.append(jnp.concatenate([late[0, at], late[1, at]], axis=1))
        total = update[i] - dot(wide, jnp.concatenate(tall, axis=0))
        leaf_res[i] = total.astype(BF16)
        return carry

    lax.fori_loop(0, LEAVES, late_leaf, 0, unroll=LEAVES)

    rest = late[zhalf, :, rows].reshape(LEVEL2 * ROWS, HALF)
    top_res[pl.ds(EARLY, LEVEL2)] = dot(rest, pick).astype(BF16).reshape(LEVEL2, ROWS, WIDTH)

    for copy in shared:
        copy.wait_send()
    others = pl.ds(0, BLOCK - ROWS)
    sent = (
        (0, inv0.at[half0, others]),
        (1, coup1.at[pairs, :, 0, pl.ds(0, SIDE - 1)]),
        (2, inv1.at[pairs, 0, pl.ds(0, SIDE - 1)]),
        (12, three_inv),
        (3, inv2.at[k, z, others]),
        (4, zbuf.at[pl.ds(0, DEPTH - 1)]),
        (5, sources.at[level0, others]),
        (6, residual.at[chunks[0], others]),
        (9, three),
        (10, sources.at[level1, others]),
        (11, residual.at[chunks[1], others]),
    )
    for g, part in sent:
        pltpu.make_async_copy(part, part, send_sem.at[g]).wait()

    pltpu.make_async_copy(seven, seven, send_sem.at[8]).wait()

    @pl.when(k != zhalf)
    def _():
        pltpu.make_async_copy(pack, pack, send_sem.at[7]).wait()


def finish(leaf_res, inverse, top_res, top_out, leaf_out, result, sem):
    last = pltpu.make_async_copy(top_res, top_out, sem.at[1])
    last.start()
    for i in range(LEAVES):
        result[i] = dot(inverse[i], leaf_res[i]).astype(BF16)
        pltpu.make_async_copy(result.at[i], leaf_out.at[i], sem.at[0]).start()
    pltpu.make_async_copy(result, leaf_out, sem.at[0]).wait()
    last.wait()


def local(
    top_sources, leaf_sources, top_inverse, leaf_inverse, top_coupling, leaf_coupling, leaf_links
):
    anywhere = pl.BlockSpec(memory_space=pltpu.HBM)
    vmem, dma = pltpu.VMEM, pltpu.SemaphoreType.DMA
    held = pl.BlockSpec(memory_space=vmem)
    top_res, leaf_res, inverse = pl.pallas_call(
        kernel,
        out_shape=(
            vmem((TOP, ROWS, WIDTH), BF16),
            vmem((LEAVES, BLOCK, BLOCK), BF16),
            vmem((LEAVES, BLOCK, BLOCK), BF16),
        ),
        in_specs=[pl.BlockSpec(memory_space=pltpu.SMEM)] + [anywhere] * 6,
        out_specs=(held, held, held),
        scratch_shapes=[
            vmem((TOP, ROWS, WIDTH), BF16),
            vmem((ROWS, BLOCK), BF16),
            vmem((8, HALF, HALF), BF16),
            vmem((DEPTH, ROWS, BLOCK), BF16),
            vmem((TOP, ROWS, HALF), BF16),
            vmem((EARLY, BLOCK, HALF), BF16),
            vmem((LEVEL0, BLOCK, BLOCK), BF16),
            vmem((LEVEL1, SIDE, SIDE, ROWS, BLOCK), BF16),
            vmem((2, LEVEL2, BLOCK, HALF), BF16),
            vmem((LEVEL1, LEVEL0, SIDE, SIDE, ROWS, BLOCK), BF16),
            vmem((LEVEL2, EARLY, ROWS, BLOCK), BF16),
            vmem((2, EARLY, BLOCK, HALF), BF16),
            vmem((2, LEVEL2, BLOCK, HALF), BF16),
            vmem((LEVEL2, ROWS, HALF), BF16),
            vmem((LEVEL2, BLOCK, HALF), BF16),
            vmem((LEAVES, LINKS, BLOCK, BLOCK), BF16),
            vmem((LEAVES, BLOCK, BLOCK), BF16),
            vmem((LEAVES, BLOCK, BLOCK), F32),
            dma((2,)),
            dma((13,)),
            dma((12,)),
            dma((7,)),
            dma((7,)),
            dma((3,)),
        ],
        compiler_params=pltpu.CompilerParams(
            collective_id=0, has_side_effects=True, vmem_limit_bytes=59 * 2**20
        ),
    )(
        leaf_links,
        top_sources,
        leaf_sources,
        top_inverse,
        leaf_inverse,
        top_coupling,
        leaf_coupling,
    )
    return pl.pallas_call(
        finish,
        out_shape=(
            jax.ShapeDtypeStruct((TOP, ROWS, WIDTH), BF16),
            jax.ShapeDtypeStruct((LEAVES, BLOCK, BLOCK), BF16),
        ),
        in_specs=[held] * 3,
        out_specs=(anywhere, anywhere),
        scratch_shapes=[vmem((LEAVES, BLOCK, BLOCK), BF16), dma((2,))],
        compiler_params=pltpu.CompilerParams(vmem_limit_bytes=16 * 2**20),
    )(leaf_res, inverse, top_res)


def solution(mesh):
    in_specs = (
        P(None, "row", "col"),
        P(("col", "row"), None, None),
        P(None, "row", None),
        P(("col", "row"), None, None),
        P(None, None, "row", None),
        P(("col", "row"), None, None, None),
        P(("col", "row"), None),
    )
    out_specs = (P(None, "row", "col"), P(("col", "row"), None, None))
    return jax.shard_map(local, mesh=mesh, in_specs=in_specs, out_specs=out_specs, check_vma=False)
```
